32 devices in a mesh: blk: 8 (over y, x, core), replica: 4 (over z).
Axes of the slice: x: 2, y: 2, z: 4, core: 2. Of those that a mesh axis runs over, the one named last changes fastest.
Arguments:
- tokens: bfloat16 [160, 4096], P('blk', 'replica'), may hold values from -6 to 6
- cotangent: bfloat16 [160, 4096], P('blk', 'replica'), may hold values from -6 to 6
- gate_weight: bfloat16 [4096, 28672], P('replica', 'blk'), may hold values from -36 to 36, as said below
- up_weight: bfloat16 [4096, 28672], P('replica', 'blk'), may hold values from -36 to 36, as said below
- down_weight: bfloat16 [28672, 4096], P('blk', 'replica'), may hold values from -72 to 72, as said below
- gate_gain: float32 [28672], P('blk'), may hold values from 0.25 to 1.75
- up_gain: float32 [28672], P('blk'), may hold values from 0.25 to 1.75
- down_gain: float32 [4096], P('replica'), may hold values from 0.25 to 1.75
Outputs:
- grad_tokens: float32 [160, 4096], P('blk', 'replica')
- grad_gate: float32 [4096, 28672], P('replica', 'blk')
- grad_up: float32 [4096, 28672], P('replica', 'blk')
- grad_down: float32 [28672, 4096], P('blk', 'replica')
- grad_gate_gain: float32 [28672], P('blk')
- grad_up_gain: float32 [28672], P('blk')
- grad_down_gain: float32 [4096], P('replica')
The draws below stay inside these ranges and needn't reach their ends.
Inputs may be any that keep to these rules, and one draw needn't show every extreme that they name: `gate_weight`: real-valued raw weights. `up_weight`: real-valued raw weights. `down_weight`: real-valued raw weights.
All inputs are finite; a program needn't handle non-finite values.
Results may differ from the reference program's by a relative error of at most 0.033.
Values may be sent and summed in bfloat16 or wider, within the bound.
A program may use at most 128 MiB of HBM per device.

```python
import jax
import jax.numpy as jnp
from jax import lax

D = 4096
FF = 28672
TOKENS = 160
N_REPLICA = 4


def rising_rows(key):
    position = jnp.arange(D, dtype=jnp.float32) / max(D - 1, 1)
    rows = jnp.exp(jnp.log(6.0) * position)
    entries = jnp.clip(jax.random.normal(jax.random.fold_in(key, 13), (D, FF), jnp.float32), -6.0, 6.0)
    value = entries * rows[:, None]
    return jnp.clip(value, -36.0, 36.0).astype(jnp.bfloat16)


def draw_gate_weight(key, part):
    return rising_rows(jax.random.fold_in(key, 101))


def draw_up_weight(key, part):
    return rising_rows(jax.random.fold_in(key, 202))


def draw_down_weight(key, part):
    base = jax.random.fold_in(key, 303)
    position = jnp.arange(FF, dtype=jnp.float32) / max(FF - 1, 1)
    offset = jax.random.uniform(jax.random.fold_in(base, 21), (D,), jnp.float32, 0.5, 1.5)
    rows = jnp.exp(jnp.log(6.0) * position)
    entries = jnp.clip(jax.random.normal(jax.random.fold_in(base, 23), (FF, D), jnp.float32), -6.0, 6.0)
    value = (entries + offset[None, :]) * rows[:, None]
    return jnp.clip(value, -72.0, 72.0).astype(jnp.bfloat16)


def block_levels(own_key, dims, pieces, low, high):
    def one(axis_at, shards_of):
        draws = jax.random.uniform(jax.random.fold_in(jax.random.fold_in(own_key, 6), axis_at), (shards_of,), jnp.float32, low / len(pieces), high / len(pieces))
        return jnp.repeat(jnp.exp(draws), dims[axis_at] // shards_of).reshape((-1,) + (1,) * (len(dims) - axis_at - 1))

    factor_of = one(*pieces[0])
    for cut in pieces[1:]:
        factor_of = factor_of * one(*cut)
    return factor_of


def gaussian(stream_key, shape, width, limit, cuts=(), kind=jnp.bfloat16):
    values = jax.random.normal(stream_key, shape, jnp.float32) * width
    if len(cuts) > 0:
        values = block_levels(stream_key, shape, cuts, -0.22, 0.18) * values
    return jnp.clip(values, min=-limit, max=limit).astype(kind)


def setup_inputs(seed: int = 0) -> dict:
    seeds = jax.random.split(jax.random.key(seed), 9)
    return {
        "tokens": gaussian(seeds[0], (TOKENS, D), 1.0, 6.0, ((0, 8), (1, 4))),
        "cotangent": gaussian(seeds[1], (TOKENS, D), 1.0, 6.0, ((0, 8), (1, 4))),
        "gate_weight": draw_gate_weight(jax.random.fold_in(seeds[8], 71), 0),
        "up_weight": draw_up_weight(jax.random.fold_in(seeds[8], 71), 0),
        "down_weight": draw_down_weight(jax.random.fold_in(seeds[8], 71), 0),
        "gate_gain": jnp.clip(1.0 + 0.15 * jax.random.normal(seeds[5], (FF,), jnp.float32), 0.25, 1.75),
        "up_gain": jnp.clip(1.0 + 0.15 * jax.random.normal(seeds[6], (FF,), jnp.float32), 0.25, 1.75),
        "down_gain": jnp.clip(1.0 + 0.15 * jax.random.normal(seeds[7], (D,), jnp.float32), 0.25, 1.75),
    }


epsilon = 0.0001
branch_scale = 0.5

def standard(weight, gain):
    raw = weight.astype(jnp.float32)
    cent = raw - lax.optimization_barrier(jnp.mean(raw, axis=0))
    scale = lax.rsqrt(lax.optimization_barrier(jnp.sum(cent * cent, axis=0)) + epsilon)
    hat = (gain.astype(jnp.float32) * cent * scale).astype(jnp.bfloat16)
    return (hat, cent, scale)

def weight_back(grad_hat, gain, cent, scale):
    count = grad_hat.shape[0]
    factor = gain.astype(jnp.float32)
    summed = lax.optimization_barrier(jnp.sum(grad_hat, axis=0))
    crossed = lax.optimization_barrier(jnp.sum(grad_hat * cent, axis=0))
    grad = scale * (factor * grad_hat - factor * summed / count) - scale * scale * scale * cent * (factor * crossed)
    return (grad, scale * crossed)

def rounded(value):
    return lax.optimization_barrier(value.astype(jnp.bfloat16)).astype(jnp.float32)

def reference(tokens, cotangent, gate_weight, up_weight, down_weight, gate_gain, up_gain, down_gain):
    gate_hat, gate_cent, gate_scale = standard(gate_weight, gate_gain)
    up_hat, up_cent, up_scale = standard(up_weight, up_gain)
    down_hat, down_cent, down_scale = standard(down_weight, down_gain)
    scaled = (branch_scale * cotangent.astype(jnp.float32)).astype(jnp.bfloat16)
    width_block = D // N_REPLICA
    gate = jnp.zeros((TOKENS, FF), jnp.float32)
    up = jnp.zeros((TOKENS, FF), jnp.float32)
    dhidden = jnp.zeros((TOKENS, FF), jnp.float32)
    for block_index in range(N_REPLICA):
        start_col = block_index * width_block
        end_col = start_col + width_block
        inputs = tokens[:, start_col:end_col]
        outward = scaled[:, start_col:end_col]
        gate = gate + rounded(jnp.dot(inputs, gate_hat[start_col:end_col], preferred_element_type=jnp.float32))
        up = up + rounded(jnp.dot(inputs, up_hat[start_col:end_col], preferred_element_type=jnp.float32))
        dhidden = dhidden + rounded(jnp.dot(outward, down_hat[:, start_col:end_col].T, preferred_element_type=jnp.float32))
    act = jax.nn.silu(gate)
    hidden = (act * up).astype(jnp.bfloat16)
    sig = jax.nn.sigmoid(gate)
    d_gate = (dhidden * up * sig * (1.0 + gate * (1.0 - sig))).astype(jnp.bfloat16)
    d_up = (dhidden * act).astype(jnp.bfloat16)
    back = jnp.dot(d_gate, gate_hat.T, preferred_element_type=jnp.float32) + jnp.dot(d_up, up_hat.T, preferred_element_type=jnp.float32)
    grad_tokens = cotangent.astype(jnp.float32) + back
    p_gate = jnp.dot(tokens.T, d_gate, preferred_element_type=jnp.float32)
    p_up = jnp.dot(tokens.T, d_up, preferred_element_type=jnp.float32)
    p_down = jnp.dot(hidden.T, scaled, preferred_element_type=jnp.float32)
    grad_gate, grad_gate_gain = weight_back(p_gate, gate_gain, gate_cent, gate_scale)
    grad_up, grad_up_gain = weight_back(p_up, up_gain, up_cent, up_scale)
    grad_down, grad_down_gain = weight_back(p_down, down_gain, down_cent, down_scale)
    return (grad_tokens, grad_gate, grad_up, grad_down, grad_gate_gain, grad_up_gain, grad_down_gain)
```

```python
import jax
import jax.numpy as jnp
from jax import lax
from jax.sharding import PartitionSpec as P

epsilon = 0.0001
branch_scale = 0.5


def contract_first(left, right):
    return lax.dot_general(
        left, right, (((0,), (0,)), ((), ())), preferred_element_type=jnp.float32
    )


def contract_last(left, right):
    return lax.dot_general(
        left, right, (((1,), (1,)), ((), ())), preferred_element_type=jnp.float32
    )


def local(tokens, cotangent, gate_weight, up_weight, down_weight, gate_gain, up_gain, down_gain):
    bf16, f32 = jnp.bfloat16, jnp.float32
    n_blk = lax.axis_size("blk")
    width_all = gate_weight.shape[0] * lax.axis_size("replica")
    hidden_all = down_weight.shape[0] * n_blk
    own, width = tokens.shape
    scaled = (branch_scale * cotangent.astype(f32)).astype(bf16)
    both = lax.all_gather(jnp.stack([tokens, scaled]), "blk", axis=0)
    whole_tokens = both[:, 0].reshape(n_blk * own, width)
    whole_scaled = both[:, 1].reshape(n_blk * own, width)
    token_sum = jnp.sum(whole_tokens.astype(f32), axis=1)

    gate_raw = gate_weight.astype(f32)
    up_raw = up_weight.astype(f32)
    gate_sum, gate_power, up_sum, up_power, token_all = lax.psum(
        (
            jnp.sum(gate_raw, axis=0),
            jnp.sum(gate_raw * gate_raw, axis=0),
            jnp.sum(up_raw, axis=0),
            jnp.sum(up_raw * up_raw, axis=0),
            token_sum,
        ),
        "replica",
    )
    gate_mean = gate_sum / width_all
    up_mean = up_sum / width_all
    gate_scale = lax.rsqrt(gate_power - gate_sum * gate_mean + epsilon)
    up_scale = lax.rsqrt(up_power - up_sum * up_mean + epsilon)
    gate_factor = gate_gain * gate_scale
    up_factor = up_gain * up_scale
    gate_part = (
        gate_factor
        * (
            jnp.dot(whole_tokens, gate_weight, preferred_element_type=f32)
            - token_sum[:, None] * gate_mean
        )
    ).astype(bf16)
    up_part = (
        up_factor
        * (
            jnp.dot(whole_tokens, up_weight, preferred_element_type=f32)
            - token_sum[:, None] * up_mean
        )
    ).astype(bf16)
    gate, up = lax.psum((gate_part, up_part), "replica")

    down_weight, _, _ = lax.optimization_barrier((down_weight, gate_part, up_part))
    down_raw = down_weight.astype(f32)
    down_sum, down_power = lax.psum(
        (jnp.sum(down_raw, axis=0), jnp.sum(down_raw * down_raw, axis=0)), "blk"
    )
    down_mean = down_sum / hidden_all
    down_scale = lax.rsqrt(down_power - down_sum * down_mean + epsilon)
    outward = (whole_scaled.astype(f32) * (down_gain * down_scale)).astype(bf16)
    outward_mean = jnp.sum(outward.astype(f32) * down_mean, axis=1)
    down_part = (contract_last(outward, down_weight) - outward_mean[:, None]).astype(bf16)
    gate, up, down_part = lax.optimization_barrier((gate, up, down_part))
    dhidden = lax.psum(down_part, "replica").astype(f32)
    gate, up = gate.astype(f32), up.astype(f32)

    sig = jax.nn.sigmoid(gate)
    act = gate * sig
    hidden = (act * up).astype(bf16)
    hidden_sum = jnp.sum(hidden.astype(f32), axis=1)
    out_part = (
        jnp.dot(hidden, down_weight, preferred_element_type=f32) - hidden_sum[:, None] * down_mean
    )
    outward32 = outward.astype(f32)
    down_psum, down_cross = lax.psum(
        (
            jnp.sum(hidden_sum[:, None] * outward32, axis=0),
            jnp.sum(outward32 * out_part, axis=0),
        ),
        "blk",
    )
    grad_down_gain = down_cross / down_gain
    down_slope = down_scale * down_scale * down_cross
    grad_down = (
        contract_first(hidden, outward)
        - down_slope * down_raw
        + (down_slope * down_mean - down_psum / hidden_all)
    )
    dhidden, grad_down, gate, up = lax.optimization_barrier((dhidden, grad_down, gate, up))
    sig = jax.nn.sigmoid(gate)
    act = gate * sig
    d_gate = dhidden * up * sig * (1.0 + gate * (1.0 - sig))
    d_up = dhidden * act
    gate_cross = jnp.sum(d_gate * gate, axis=0)
    up_cross = jnp.sum(d_up * up, axis=0)
    gate_back = (d_gate * gate_factor).astype(bf16)
    up_back = (d_up * up_factor).astype(bf16)
    back_mean = jnp.sum(gate_back.astype(f32) * gate_mean + up_back.astype(f32) * up_mean, axis=1)
    back = (
        contract_last(gate_back, gate_weight)
        + contract_last(up_back, up_weight)
        - back_mean[:, None]
    ).astype(bf16)
    pieces = lax.all_to_all(
        back.reshape(n_blk, own, width), "blk", split_axis=0, concat_axis=0, tiled=True
    )
    grad_tokens = cotangent.astype(f32) + jnp.sum(pieces.astype(f32), axis=0)

    grad_gate_gain = gate_cross / gate_gain
    grad_up_gain = up_cross / up_gain
    gate_slope = gate_scale * gate_scale * gate_cross
    up_slope = up_scale * up_scale * up_cross
    gate_psum = jnp.sum(token_all[:, None] * gate_back.astype(f32), axis=0)
    up_psum = jnp.sum(token_all[:, None] * up_back.astype(f32), axis=0)
    grad_gate = (
        contract_first(whole_tokens, gate_back)
        - gate_slope * gate_raw
        + (gate_slope * gate_mean - gate_psum / width_all)
    )
    grad_up = (
        contract_first(whole_tokens, up_back)
        - up_slope * up_raw
        + (up_slope * up_mean - up_psum / width_all)
    )
    return (
        grad_tokens,
        grad_gate,
        grad_up,
        grad_down,
        grad_gate_gain,
        grad_up_gain,
        grad_down_gain,
    )


def solution(mesh):
    return jax.shard_map(
        local,
        mesh=mesh,
        in_specs=(
            P("blk", "replica"),
            P("blk", "replica"),
            P("replica", "blk"),
            P("replica", "blk"),
            P("blk", "replica"),
            P("blk"),
            P("blk"),
            P("replica"),
        ),
        out_specs=(
            P("blk", "replica"),
            P("replica", "blk"),
            P("replica", "blk"),
            P("blk", "replica"),
            P("blk"),
            P("blk"),
            P("replica"),
        ),
        check_vma=False,
    )
```

```python
import jax
import jax.numpy as jnp
from jax import lax
from jax.sharding import PartitionSpec as P

epsilon = 0.0001
branch_scale = 0.5


def contract_first(left, right):
    return lax.dot_general(
        left, right, (((0,), (0,)), ((), ())), preferred_element_type=jnp.float32
    )


def contract_last(left, right):
    return lax.dot_general(
        left, right, (((1,), (1,)), ((), ())), preferred_element_type=jnp.float32
    )


def shift(left, right):
    return lax.dot_general(
        left,
        right,
        (((0,), (0,)), ((), ())),
        precision=lax.Precision.HIGHEST,
        preferred_element_type=jnp.float32,
    )


def local(tokens, cotangent, gate_weight, up_weight, down_weight, gate_gain, up_gain, down_gain):
    bf16, f32 = jnp.bfloat16, jnp.float32
    n_blk = lax.axis_size("blk")
    width_all = gate_weight.shape[0] * lax.axis_size("replica")
    hidden_all = down_weight.shape[0] * n_blk
    own, width = tokens.shape
    scaled = (branch_scale * cotangent.astype(f32)).astype(bf16)
    both = lax.all_gather(jnp.stack([tokens, scaled]), "blk", axis=0)
    whole_tokens = both[:, 0].reshape(n_blk * own, width)
    whole_scaled = both[:, 1].reshape(n_blk * own, width)
    token_sum = jnp.sum(whole_tokens.astype(f32), axis=1)

    gate_raw = gate_weight.astype(f32)
    up_raw = up_weight.astype(f32)
    block = gate_weight.shape[0]
    hidden_own = gate_weight.shape[1]
    sums = (
        jnp.sum(gate_raw, axis=0),
        jnp.sum(gate_raw * gate_raw, axis=0),
        jnp.sum(up_raw, axis=0),
        jnp.sum(up_raw * up_raw, axis=0),
    )
    gate_part = (
        jnp.dot(whole_tokens, gate_weight, preferred_element_type=f32)
        - token_sum[:, None] * (sums[0] / block)
    ).astype(bf16)
    up_part = (
        jnp.dot(whole_tokens, up_weight, preferred_element_type=f32)
        - token_sum[:, None] * (sums[2] / block)
    ).astype(bf16)
    gate, up = lax.psum((gate_part, up_part), "replica")

    lanes = jnp.concatenate(sums + (token_sum,))
    lanes = jnp.pad(lanes, (0, -lanes.shape[0] % 1024)).reshape(-1, 128)
    lanes, _, _ = lax.optimization_barrier((lanes, gate_part, up_part))
    lanes = lax.all_gather(lanes, "replica", axis=0)
    stats = lanes.reshape(lanes.shape[0], -1)
    gate_sums = stats[:, :hidden_own]
    up_sums = stats[:, 2 * hidden_own : 3 * hidden_own]
    token_sums = stats[:, 4 * hidden_own : 4 * hidden_own + n_blk * own]
    gate_power = jnp.sum(stats[:, hidden_own : 2 * hidden_own], axis=0)
    up_power = jnp.sum(stats[:, 3 * hidden_own : 4 * hidden_own], axis=0)
    gate_sum = jnp.sum(gate_sums, axis=0)
    up_sum = jnp.sum(up_sums, axis=0)
    token_all = jnp.sum(token_sums, axis=0)
    gate_mean = gate_sum / width_all
    up_mean = up_sum / width_all
    gate_scale = lax.rsqrt(gate_power - gate_sum * gate_mean + epsilon)
    up_scale = lax.rsqrt(up_power - up_sum * up_mean + epsilon)
    gate_factor = gate_gain * gate_scale
    up_factor = up_gain * up_scale
    gate_shift = shift(token_sums, gate_sums / block - gate_mean)
    up_shift = shift(token_sums, up_sums / block - up_mean)

    down_weight, _, _ = lax.optimization_barrier((down_weight, gate_part, up_part))
    down_raw = down_weight.astype(f32)
    down_sum, down_power = lax.psum(
        (jnp.sum(down_raw, axis=0), jnp.sum(down_raw * down_raw, axis=0)), "blk"
    )
    down_mean = down_sum / hidden_all
    down_scale = lax.rsqrt(down_power - down_sum * down_mean + epsilon)
    outward = (whole_scaled.astype(f32) * (down_gain * down_scale)).astype(bf16)
    outward_mean = jnp.sum(outward.astype(f32) * down_mean, axis=1)
    down_part = (contract_last(outward, down_weight) - outward_mean[:, None]).astype(bf16)
    gate, up, down_part, gate_shift, up_shift = lax.optimization_barrier(
        (gate, up, down_part, gate_shift, up_shift)
    )
    dhidden = lax.psum(down_part, "replica").astype(f32)
    gate = gate_factor * (gate.astype(f32) + gate_shift)
    up = up_factor * (up.astype(f32) + up_shift)

    sig = jax.nn.sigmoid(gate)
    act = gate * sig
    hidden = (act * up).astype(bf16)
    hidden_sum = jnp.sum(hidden.astype(f32), axis=1)
    out_part = (
        jnp.dot(hidden, down_weight, preferred_element_type=f32) - hidden_sum[:, None] * down_mean
    )
    outward32 = outward.astype(f32)
    down_psum, down_cross = lax.psum(
        (
            jnp.sum(hidden_sum[:, None] * outward32, axis=0),
            jnp.sum(outward32 * out_part, axis=0),
        ),
        "blk",
    )
    grad_down_gain = down_cross / down_gain
    down_slope = down_scale * down_scale * down_cross
    grad_down = (
        contract_first(hidden, outward)
        - down_slope * down_raw
        + (down_slope * down_mean - down_psum / hidden_all)
    )
    dhidden, grad_down, gate, up = lax.optimization_barrier((dhidden, grad_down, gate, up))
    sig = jax.nn.sigmoid(gate)
    act = gate * sig
    d_gate = dhidden * up * sig * (1.0 + gate * (1.0 - sig))
    d_up = dhidden * act
    gate_cross = jnp.sum(d_gate * gate, axis=0)
    up_cross = jnp.sum(d_up * up, axis=0)
    gate_back = (d_gate * gate_factor).astype(bf16)
    up_back = (d_up * up_factor).astype(bf16)
    back_mean = jnp.sum(gate_back.astype(f32) * gate_mean + up_back.astype(f32) * up_mean, axis=1)
    back = (
        contract_last(gate_back, gate_weight)
        + contract_last(up_back, up_weight)
        - back_mean[:, None]
    ).astype(bf16)
    pieces = lax.all_to_all(
        back.reshape(n_blk, own, width), "blk", split_axis=0, concat_axis=0, tiled=True
    )
    grad_tokens = cotangent.astype(f32) + jnp.sum(pieces.astype(f32), axis=0)

    grad_gate_gain = gate_cross / gate_gain
    grad_up_gain = up_cross / up_gain
    gate_slope = gate_scale * gate_scale * gate_cross
    up_slope = up_scale * up_scale * up_cross
    gate_psum = jnp.sum(token_all[:, None] * gate_back.astype(f32), axis=0)
    up_psum = jnp.sum(token_all[:, None] * up_back.astype(f32), axis=0)
    grad_gate = (
        contract_first(whole_tokens, gate_back)
        - gate_slope * gate_raw
        + (gate_slope * gate_mean - gate_psum / width_all)
    )
    grad_up = (
        contract_first(whole_tokens, up_back)
        - up_slope * up_raw
        + (up_slope * up_mean - up_psum / width_all)
    )
    return (
        grad_tokens,
        grad_gate,
        grad_up,
        grad_down,
        grad_gate_gain,
        grad_up_gain,
        grad_down_gain,
    )


def solution(mesh):
    return jax.shard_map(
        local,
        mesh=mesh,
        in_specs=(
            P("blk", "replica"),
            P("blk", "replica"),
            P("replica", "blk"),
            P("replica", "blk"),
            P("blk", "replica"),
            P("blk"),
            P("blk"),
            P("replica"),
        ),
        out_specs=(
            P("blk", "replica"),
            P("replica", "blk"),
            P("replica", "blk"),
            P("blk", "replica"),
            P("blk"),
            P("blk"),
            P("replica"),
        ),
        check_vma=False,
    )
```
